32 devices in a mesh: row: 8 (over z, y), col: 4 (over x, core).
Axes of the slice: x: 2, y: 2, z: 4, core: 2. Of those that a mesh axis runs over, the one named last changes fastest.
Arguments:
- weight: bfloat16 [16384, 32768], P('row', 'col'), may hold values from -600 to 600
- basis_prev: bfloat16 [32768, 512], P(('col', 'row')), may hold values from -6 to 6
Outputs:
- left_basis: bfloat16 [16384, 512], P(('row', 'col'))
- right_factor: bfloat16 [32768, 512], P(('col', 'row'))
The draws below stay inside these ranges and needn't reach their ends.
All inputs are finite; a program needn't handle non-finite values.
Results may differ from the reference program's by a relative error of at most 0.0042.
Values may be sent and summed in bfloat16 or wider, within the bound.
A program may use at most 128 MiB of HBM per device.

```python
import jax
import jax.numpy as jnp
from jax import lax

D = 16384
FF = 32768
R = 512


def draw_weight(key, part):
    key = jax.random.fold_in(key, 11)
    key_base, key_rows, key_cols = jax.random.split(key, 3)
    position = jnp.arange(D, dtype=jnp.float32) / jnp.float32(D)
    row_noise = jax.random.uniform(key_rows, (D,), jnp.float32)
    col_noise = jax.random.uniform(key_cols, (FF,), jnp.float32)
    base = jnp.clip(jax.random.normal(key_base, (D, FF), jnp.float32), -6.0, 6.0)
    row_scale = 10.0 ** (0.5 * position + 0.5 * row_noise)
    col_scale = 10.0 ** col_noise
    return (base * row_scale[:, None] * col_scale[None, :]).astype(jnp.bfloat16)


def level_of(stream_key, dims, cuts, least, top_value):
    level, own = 1.0, jax.random.fold_in(stream_key, 6)
    for dim, blocks in cuts:
        draws = jnp.exp(jax.random.uniform(jax.random.fold_in(own, dim), (blocks,), jnp.float32, least / len(cuts), top_value / len(cuts)))
        level = level * jnp.repeat(draws, dims[dim] // blocks).reshape([-1 if axis == dim else 1 for axis in range(len(dims))])
    return level


def scatter_about(own_key, extent, deviation, bound, shards=(), kind=jnp.bfloat16):
    entries = deviation * jax.random.normal(own_key, extent, jnp.float32)
    if shards:
        entries = entries * level_of(own_key, extent, shards, -0.22, 0.18)
    return jnp.clip(entries, -bound, bound).astype(kind)


def setup_inputs(seed: int = 0) -> dict:
    splits = jax.random.split(jax.random.key(seed), 3)
    weight = draw_weight(jax.random.fold_in(splits[2], 71), 0)
    basis_prev = scatter_about(splits[1], (FF, R), 1.0, 6.0, ((0, 32),))
    return dict(weight=weight, basis_prev=basis_prev)


def reference(weight, basis_prev):
    sketch = jnp.dot(weight.astype(jnp.float32), basis_prev.astype(jnp.float32), preferred_element_type=jnp.float32)
    gram = jnp.dot(sketch.T.astype(jnp.float32), sketch.astype(jnp.float32), precision=lax.Precision.HIGHEST, preferred_element_type=jnp.float32) / jnp.float32(D)
    lower = jnp.linalg.cholesky(gram)
    solved = lax.linalg.triangular_solve(lower, sketch, left_side=False, lower=True, transpose_a=True)
    left_basis = solved.astype(jnp.bfloat16)
    product = jnp.dot(weight.T.astype(jnp.float32), left_basis.astype(jnp.float32), preferred_element_type=jnp.float32)
    right_factor = (product * jnp.float32(D ** (-0.5))).astype(jnp.bfloat16)
    return (left_basis, right_factor)
```

```python
import jax
import jax.numpy as jnp
from jax import lax
from jax.sharding import PartitionSpec as P

F32 = jnp.float32
BF16 = jnp.bfloat16
HIGH = lax.Precision.HIGHEST


def dot(a, b, dims, precision=None):
    return lax.dot_general(a, b, ((dims[0], dims[1]), ((), ())), precision=precision,
                           preferred_element_type=F32)


def pair_of(n):
    return [(i, i ^ 1) for i in range(n)]


def ring_of(n):
    return [(i, (i + 2) % n) for i in range(n)]


def rows_of(x, start, count):
    return lax.dynamic_slice_in_dim(x, start, count, 0)


def all_sum(gram, sizes):
    steps = []
    held = gram
    for axis, n in sizes:
        bit = 1
        while bit < n:
            half = held.shape[0] // 2
            mine = (lax.axis_index(axis) // bit) % 2
            pairs = [(i, i ^ bit) for i in range(n)]
            got = lax.ppermute(rows_of(held, (1 - mine) * half, half), axis, pairs)
            held = rows_of(held, mine * half, half) + got
            steps.append((axis, pairs, mine))
            bit *= 2
    for axis, pairs, mine in reversed(steps):
        got = lax.ppermute(held, axis, pairs)
        low = jnp.where(mine == 0, held, got)
        high = jnp.where(mine == 0, got, held)
        held = jnp.concatenate([low, high], 0)
    return held


def inverse_factor(gram):
    n = gram.shape[0]
    b = 128
    eye = jnp.eye(b, dtype=F32)
    rest = gram
    rows = []
    panels = []
    count = n // b
    for i in range(count):
        head = rest[:b, :b]
        low = lax.linalg.cholesky(head, symmetrize_input=False)
        inv = lax.linalg.triangular_solve(low, eye, left_side=True, lower=True)
        if i + 1 < count:
            panel = dot(rest[b:, :b], inv, ((1,), (1,)), HIGH)
            rest = rest[b:, b:] - dot(panel, panel, ((1,), (1,)), HIGH)
            panels.append(panel)
        left = jnp.zeros((b, i * b), F32)
        if i:
            own = jnp.concatenate([panels[j][(i - 1 - j) * b:(i - j) * b] for j in range(i)], 1)
            left = -dot(inv, dot(own, jnp.concatenate(rows, 0)[:, :i * b], ((1,), (0,)), HIGH),
                        ((1,), (0,)), HIGH)
        rows.append(jnp.concatenate([left, inv, jnp.zeros((b, n - (i + 1) * b), F32)], 1))
    return jnp.concatenate(rows, 0)


def per_device(n_row, n_col, d, weight, basis_prev):
    depth, rank = basis_prev.shape
    me = lax.axis_index("row")
    group, side = me // 2, me % 2
    ring = n_row // 2

    held = basis_prev
    partial = None
    for step in range(ring):
        other = lax.ppermute(held, "row", pair_of(n_row))
        later = lax.ppermute(held, "row", ring_of(n_row)) if step + 1 < ring else None
        owner = (group - step + ring) % ring
        both = jnp.concatenate([jnp.where(side == 0, held, other), jnp.where(side == 0, other, held)], 0)
        cut = lax.dynamic_slice_in_dim(weight, owner * 2 * depth, 2 * depth, 1)
        term = dot(cut, both, ((1,), (0,)))
        partial = term if partial is None else partial + term
        held = later

    rows = weight.shape[0] // n_col
    col = lax.axis_index("col")
    cgroup, cside = col // 2, col % 2
    cring = n_col // 2
    parts = partial.reshape(cring, 2, rows, rank)
    away = lax.dynamic_index_in_dim(parts, 1 - cside, 1, keepdims=False)
    near = lax.dynamic_index_in_dim(parts, cside, 1, keepdims=False)
    near = near + lax.ppermute(away, "col", pair_of(n_col))
    sketch = None
    for step in range(cring):
        at = (cgroup - 1 - step + 2 * cring) % cring
        own = lax.dynamic_index_in_dim(near, at, 0, keepdims=False)
        sketch = own if sketch is None else own + sketch.astype(F32)
        if step + 1 < cring:
            sketch = lax.ppermute(sketch.astype(BF16), "col", ring_of(n_col))

    full = jnp.zeros((cring, 2, rows, rank), BF16)
    held = sketch.astype(BF16)
    for step in range(cring):
        other = lax.ppermute(held, "col", pair_of(n_col))
        later = lax.ppermute(held, "col", ring_of(n_col)) if step + 1 < cring else None
        two = jnp.stack([jnp.where(cside == 0, held, other), jnp.where(cside == 0, other, held)])
        full = lax.dynamic_update_slice(full, two[None], ((cgroup - step + cring) % cring, 0, 0, 0))
        held = later
    full = full.reshape(n_col * rows, rank)

    gram = dot(sketch, sketch, ((0,), (0,)), HIGH)
    gram = all_sum(gram, (("col", n_col), ("row", n_row)))
    inverse = inverse_factor(gram / F32(d))

    factor = None
    for step in range(ring):
        at = (group - 1 - step + 2 * ring) % ring
        cut = lax.dynamic_slice_in_dim(weight, at * 2 * depth, 2 * depth, 1)
        term = dot(cut, full, ((0,), (0,)))
        got = lax.ppermute(rows_of(term, (1 - side) * depth, depth).astype(BF16), "row", pair_of(n_row))
        term = rows_of(term, side * depth, depth) + got.astype(F32)
        factor = term if factor is None else term + factor.astype(F32)
        if step + 1 < ring:
            factor = lax.ppermute(factor.astype(BF16), "row", ring_of(n_row))

    left_basis = dot(sketch, inverse, ((1,), (1,)), HIGH).astype(BF16)
    right = dot(factor, inverse, ((1,), (1,)), HIGH)
    return left_basis, (right * F32(d ** (-0.5))).astype(BF16)


def solution(mesh):
    n_row, n_col = mesh.shape["row"], mesh.shape["col"]

    def run(weight, basis_prev):
        def body(w, b):
            return per_device(n_row, n_col, weight.shape[0], w, b)

        return jax.shard_map(
            body,
            mesh=mesh,
            in_specs=(P("row", "col"), P(("col", "row"), None)),
            out_specs=(P(("row", "col"), None), P(("col", "row"), None)),
            check_vma=False,
        )(weight, basis_prev)

    return run
```

```python
import jax
import jax.numpy as jnp
from jax import lax
from jax.experimental import pallas as pl
from jax.experimental.pallas import tpu as pltpu
from jax.sharding import PartitionSpec as P

F32 = jnp.float32
BF16 = jnp.bfloat16
HIGH = lax.Precision.HIGHEST


def dot(a, b, dims, precision=None):
    return lax.dot_general(a, b, ((dims[0], dims[1]), ((), ())), precision=precision,
                           preferred_element_type=F32)


def pair_of(n):
    return [(i, i ^ 1) for i in range(n)]


def ring_of(n):
    return [(i, (i + 2) % n) for i in range(n)]


def rows_of(x, start, count):
    return lax.dynamic_slice_in_dim(x, start, count, 0)


def all_sum(gram, sizes):
    steps = []
    held = gram
    for axis, n in sizes:
        bit = 1
        while bit < n:
            half = held.shape[0] // 2
            mine = (lax.axis_index(axis) // bit) % 2
            pairs = [(i, i ^ bit) for i in range(n)]
            got = lax.ppermute(rows_of(held, (1 - mine) * half, half), axis, pairs)
            held = rows_of(held, mine * half, half) + got
            steps.append((axis, pairs, mine))
            bit *= 2
    for axis, pairs, mine in reversed(steps):
        got = lax.ppermute(held, axis, pairs)
        low = jnp.where(mine == 0, held, got)
        high = jnp.where(mine == 0, got, held)
        held = jnp.concatenate([low, high], 0)
    return held


def inverse_kernel(gram_ref, out_ref, work_ref, aug_ref):
    n, b, w = gram_ref.shape[0], 128, 4
    work_ref[...] = gram_ref[...]
    aug_ref[...] = (
        lax.broadcasted_iota(jnp.int32, (n, n), 0) == lax.broadcasted_iota(jnp.int32, (n, n), 1)
    ).astype(F32)
    lane = lax.broadcasted_iota(jnp.int32, (8, b), 1)
    sub = lax.broadcasted_iota(jnp.int32, (8, b), 0)

    def block(i, carry):
        at = pl.ds(pl.multiple_of(i * b, b), b)
        x = [work_ref[pl.ds(pl.multiple_of(i * b + 8 * g, 8), 8), at] for g in range(b // 8)]
        for base in range(0, b, w):
            first = base // 8
            groups = range(first, b // 8)
            wide = {
                (j, g): jnp.broadcast_to(x[g][:, j:j + 1], (8, b))
                for j in range(base, base + w) for g in groups
            }
            for k in range(base, base + w):
                s = k % 8
                over = 1.0 / wide[k, first][s:s + 1]
                row = jnp.where(lane[:1] == k, 1.0, x[first][s:s + 1]) * over
                heads = {j: wide[j, first][s:s + 1] * over for j in range(k + 1, base + w)}
                for g in groups:
                    c = wide[k, g]
                    gone = lane == k
                    if g == first:
                        c = jnp.where(sub > s, c, 0.0)
                        gone = gone & (sub > s)
                    x[g] = jnp.where(gone, 0.0, x[g]) - c * row
                    for j, head in heads.items():
                        wide[j, g] = wide[j, g] - c * head
        rows = []
        for g in range(b // 8):
            here = lane == sub + 8 * g
            pivot = jnp.sum(jnp.where(here, x[g], 0.0), axis=1, keepdims=True)
            unit = jnp.where(lane < sub + 8 * g, x[g], jnp.where(here, 1.0, 0.0))
            rows.append(unit / jnp.sqrt(pivot))
        inv = jnp.concatenate(rows, 0)
        head = dot(inv, work_ref[at, :], ((1,), (0,)), HIGH)
        tail = dot(inv, aug_ref[at, :], ((1,), (0,)), HIGH)
        out_ref[at, :] = tail
        work_ref[...] -= dot(head, head, ((0,), (0,)), HIGH)
        aug_ref[...] -= dot(head, tail, ((0,), (0,)), HIGH)
        return carry

    lax.fori_loop(0, n // b, block, 0)


def inverse_factor(gram):
    n = gram.shape[0]
    return pl.pallas_call(
        inverse_kernel,
        out_shape=jax.ShapeDtypeStruct((n, n), F32),
        in_specs=[pl.BlockSpec(memory_space=pltpu.VMEM)],
        out_specs=pl.BlockSpec(memory_space=pltpu.VMEM),
        scratch_shapes=[pltpu.VMEM((n, n), F32), pltpu.VMEM((n, n), F32)],
        cost_estimate=pl.CostEstimate(flops=20_000_000_000, bytes_accessed=8 * n * n, transcendentals=0),
        compiler_params=pltpu.CompilerParams(vmem_limit_bytes=24 * 2**20),
    )(gram)


def per_device(n_row, n_col, d, weight, basis_prev):
    depth, rank = basis_prev.shape
    me = lax.axis_index("row")
    group, side = me // 2, me % 2
    ring = n_row // 2
    down_ring = [(j, i) for i, j in ring_of(n_row)]

    held = basis_prev
    partial = None
    for step in range(ring):
        other = lax.ppermute(held, "row", pair_of(n_row))
        later = lax.ppermute(held, "row", ring_of(n_row)) if step + 1 < ring else None
        owner = (group - step + ring) % ring
        if step + 1 < ring:
            both = jnp.concatenate(
                [jnp.where(side == 0, held, other), jnp.where(side == 0, other, held)], 0)
            cut = lax.dynamic_slice_in_dim(weight, owner * 2 * depth, 2 * depth, 1)
            term = dot(cut, both, ((1,), (0,)))
            partial = term if partial is None else partial + term
        else:
            cut = lax.dynamic_slice_in_dim(weight, (owner * 2 + side) * depth, depth, 1)
            partial = partial + dot(cut, held, ((1,), (0,)))
            partial, other = lax.optimization_barrier((partial, other))
            cut = lax.dynamic_slice_in_dim(weight, (owner * 2 + 1 - side) * depth, depth, 1)
            partial = partial + dot(cut, other, ((1,), (0,)))
        held = later

    rows = weight.shape[0] // n_col
    col = lax.axis_index("col")
    cgroup, cside = col // 2, col % 2
    cring = n_col // 2
    parts = partial.reshape(cring, 2, rows, rank)
    away = lax.dynamic_index_in_dim(parts, 1 - cside, 1, keepdims=False)
    near = lax.dynamic_index_in_dim(parts, cside, 1, keepdims=False)
    near = near + lax.ppermute(away, "col", pair_of(n_col))
    sketch = None
    for step in range(cring):
        at = (cgroup - 1 - step + 2 * cring) % cring
        own = lax.dynamic_index_in_dim(near, at, 0, keepdims=False)
        sketch = own if sketch is None else own + sketch.astype(F32)
        if step + 1 < cring:
            sketch = lax.ppermute(sketch.astype(BF16), "col", ring_of(n_col))

    full = jnp.zeros((cring, 2, rows, rank), BF16)
    held = sketch.astype(BF16)
    for step in range(cring):
        other = lax.ppermute(held, "col", pair_of(n_col))
        later = lax.ppermute(held, "col", ring_of(n_col)) if step + 1 < cring else None
        two = jnp.stack([jnp.where(cside == 0, held, other), jnp.where(cside == 0, other, held)])
        full = lax.dynamic_update_slice(full, two[None], ((cgroup - step + cring) % cring, 0, 0, 0))
        held = later
    full = full.reshape(n_col * rows, rank)

    gram = dot(sketch, sketch, ((0,), (0,)), HIGH)
    full, gram = lax.optimization_barrier((full, gram))
    gram = all_sum(gram, (("row", n_row), ("col", n_col)))
    inverse = inverse_factor(gram / F32(d))

    def factor_of(at):
        cut = lax.dynamic_slice_in_dim(weight, at * 2 * depth, 2 * depth, 1)
        term = dot(cut, full, ((0,), (0,)))
        away = rows_of(term, (1 - side) * depth, depth).astype(BF16)
        return rows_of(term, side * depth, depth), lax.ppermute(away, "row", pair_of(n_row))

    up_hops = ring // 2
    down_hops = ring - 1 - up_hops
    order = []
    for step in range(up_hops):
        order.append(up_hops - step)
        if step < down_hops:
            order.append(step - down_hops)
    order.append(0)
    terms = {at: factor_of((group + at + ring) % ring) for at in order}

    def travel(hops, sign, pairs):
        moving = None
        for step in range(hops):
            own, got = terms[sign * (hops - step)]
            own = own + got.astype(F32)
            if moving is not None:
                own = own + moving.astype(F32)
            moving = lax.ppermute(own.astype(BF16), "row", pairs)
        return moving

    up = travel(up_hops, 1, ring_of(n_row))
    down = travel(down_hops, -1, down_ring)
    factor, got = terms[0]
    factor = factor + got.astype(F32)
    for moved in (up, down):
        if moved is not None:
            factor = factor + moved.astype(F32)

    left_basis = dot(sketch, inverse, ((1,), (1,)), HIGH).astype(BF16)
    right = dot(factor, inverse, ((1,), (1,)), HIGH)
    return left_basis, (right * F32(d ** (-0.5))).astype(BF16)


def solution(mesh):
    n_row, n_col = mesh.shape["row"], mesh.shape["col"]

    def run(weight, basis_prev):
        def body(w, b):
            return per_device(n_row, n_col, weight.shape[0], w, b)

        return jax.shard_map(
            body,
            mesh=mesh,
            in_specs=(P("row", "col"), P(("col", "row"), None)),
            out_specs=(P(("row", "col"), None), P(("col", "row"), None)),
            check_vma=False,
        )(weight, basis_prev)

    return run
```

```python
import jax
import jax.numpy as jnp
from jax import lax
from jax.experimental import pallas as pl
from jax.experimental.pallas import tpu as pltpu
from jax.sharding import PartitionSpec as P

F32 = jnp.float32
BF16 = jnp.bfloat16
HIGH = lax.Precision.HIGHEST


def dot(a, b, dims, precision=None):
    return lax.dot_general(a, b, ((dims[0], dims[1]), ((), ())), precision=precision,
                           preferred_element_type=F32)


def pair_of(n):
    return [(i, i ^ 1) for i in range(n)]


def ring_of(n):
    return [(i, (i + 2) % n) for i in range(n)]


def rows_of(x, start, count):
    return lax.dynamic_slice_in_dim(x, start, count, 0)


def all_sum(gram, sizes):
    steps = []
    held = gram
    for axis, n in sizes:
        bit = 1
        while bit < n:
            half = held.shape[0] // 2
            mine = (lax.axis_index(axis) // bit) % 2
            pairs = [(i, i ^ bit) for i in range(n)]
            got = lax.ppermute(rows_of(held, (1 - mine) * half, half), axis, pairs)
            held = rows_of(held, mine * half, half) + got
            steps.append((axis, pairs, mine))
            bit *= 2
    for axis, pairs, mine in reversed(steps):
        got = lax.ppermute(held, axis, pairs)
        low = jnp.where(mine == 0, held, got)
        high = jnp.where(mine == 0, got, held)
        held = jnp.concatenate([low, high], 0)
    return held


def inverse_kernel(gram_ref, out_ref, work_ref, aug_ref):
    n, b, w = gram_ref.shape[0], 128, 4
    work_ref[...] = gram_ref[...]
    aug_ref[...] = (
        lax.broadcasted_iota(jnp.int32, (n, n), 0) == lax.broadcasted_iota(jnp.int32, (n, n), 1)
    ).astype(F32)
    lane = lax.broadcasted_iota(jnp.int32, (8, b), 1)
    sub = lax.broadcasted_iota(jnp.int32, (8, b), 0)

    def block(i, carry):
        at = pl.ds(pl.multiple_of(i * b, b), b)
        x = [work_ref[pl.ds(pl.multiple_of(i * b + 8 * g, 8), 8), at] for g in range(b // 8)]
        for base in range(0, b, w):
            first = base // 8
            groups = range(first, b // 8)
            wide = {
                (j, g): jnp.broadcast_to(x[g][:, j:j + 1], (8, b))
                for j in range(base, base + w) for g in groups
            }
            for k in range(base, base + w):
                s = k % 8
                over = 1.0 / wide[k, first][s:s + 1]
                row = jnp.where(lane[:1] == k, 1.0, x[first][s:s + 1]) * over
                heads = {j: wide[j, first][s:s + 1] * over for j in range(k + 1, base + w)}
                for g in groups:
                    c = wide[k, g]
                    gone = lane == k
                    if g == first:
                        c = jnp.where(sub > s, c, 0.0)
                        gone = gone & (sub > s)
                    x[g] = jnp.where(gone, 0.0, x[g]) - c * row
                    for j, head in heads.items():
                        wide[j, g] = wide[j, g] - c * head
        rows = []
        for g in range(b // 8):
            here = lane == sub + 8 * g
            pivot = jnp.sum(jnp.where(here, x[g], 0.0), axis=1, keepdims=True)
            unit = jnp.where(lane < sub + 8 * g, x[g], jnp.where(here, 1.0, 0.0))
            rows.append(unit / jnp.sqrt(pivot))
        inv = jnp.concatenate(rows, 0)
        head = dot(inv, work_ref[at, :], ((1,), (0,)), HIGH)
        tail = dot(inv, aug_ref[at, :], ((1,), (0,)), HIGH)
        out_ref[at, :] = tail
        work_ref[...] -= dot(head, head, ((0,), (0,)), HIGH)
        aug_ref[...] -= dot(head, tail, ((0,), (0,)), HIGH)
        return carry

    lax.fori_loop(0, n // b, block, 0)


def inverse_factor(gram):
    n = gram.shape[0]
    return pl.pallas_call(
        inverse_kernel,
        out_shape=jax.ShapeDtypeStruct((n, n), F32),
        in_specs=[pl.BlockSpec(memory_space=pltpu.VMEM)],
        out_specs=pl.BlockSpec(memory_space=pltpu.VMEM),
        scratch_shapes=[pltpu.VMEM((n, n), F32), pltpu.VMEM((n, n), F32)],
        cost_estimate=pl.CostEstimate(flops=20_000_000_000, bytes_accessed=8 * n * n, transcendentals=0),
        compiler_params=pltpu.CompilerParams(vmem_limit_bytes=24 * 2**20),
    )(gram)


def per_device(n_row, n_col, d, weight, basis_prev):
    depth, rank = basis_prev.shape
    me = lax.axis_index("row")
    group, side = me // 2, me % 2
    ring = n_row // 2
    down_ring = [(j, i) for i, j in ring_of(n_row)]

    held = basis_prev
    partial = other = None
    half = depth // 2
    for step in range(ring):
        if step and step + 1 == ring:
            first = lax.ppermute(held[:half], "row", pair_of(n_row))
            second = lax.ppermute(other[half:], "row", ring_of(n_row))
            other = jnp.concatenate([first, second], 0)
        else:
            other = lax.ppermute(held, "row", pair_of(n_row))
        later = lax.ppermute(held, "row", ring_of(n_row)) if step + 1 < ring else None
        owner = (group - step + ring) % ring
        if step + 1 < ring:
            both = jnp.concatenate(
                [jnp.where(side == 0, held, other), jnp.where(side == 0, other, held)], 0)
            cut = lax.dynamic_slice_in_dim(weight, owner * 2 * depth, 2 * depth, 1)
            term = dot(cut, both, ((1,), (0,)))
            partial = term if partial is None else partial + term
        else:
            cut = lax.dynamic_slice_in_dim(weight, (owner * 2 + side) * depth, depth, 1)
            partial = partial + dot(cut, held, ((1,), (0,)))
            partial, other = lax.optimization_barrier((partial, other))
            cut = lax.dynamic_slice_in_dim(weight, (owner * 2 + 1 - side) * depth, depth, 1)
            partial = partial + dot(cut, other, ((1,), (0,)))
        held = later

    rows = weight.shape[0] // n_col
    col = lax.axis_index("col")
    cgroup, cside = col // 2, col % 2
    cring = n_col // 2
    parts = partial.reshape(cring, 2, rows, rank)
    away = lax.dynamic_index_in_dim(parts, 1 - cside, 1, keepdims=False)
    near = lax.dynamic_index_in_dim(parts, cside, 1, keepdims=False)
    near = near + lax.ppermute(away, "col", pair_of(n_col))
    sketch = None
    for step in range(cring):
        at = (cgroup - 1 - step + 2 * cring) % cring
        own = lax.dynamic_index_in_dim(near, at, 0, keepdims=False)
        sketch = own if sketch is None else own + sketch.astype(F32)
        if step + 1 < cring:
            sketch = lax.ppermute(sketch.astype(BF16), "col", ring_of(n_col))

    full = jnp.zeros((cring, 2, rows, rank), BF16)
    held = sketch.astype(BF16)
    for step in range(cring):
        other = lax.ppermute(held, "col", pair_of(n_col))
        later = lax.ppermute(held, "col", ring_of(n_col)) if step + 1 < cring else None
        two = jnp.stack([jnp.where(cside == 0, held, other), jnp.where(cside == 0, other, held)])
        full = lax.dynamic_update_slice(full, two[None], ((cgroup - step + cring) % cring, 0, 0, 0))
        held = later
    full = full.reshape(n_col * rows, rank)

    gram = dot(sketch, sketch, ((0,), (0,)), HIGH)
    full, gram = lax.optimization_barrier((full, gram))
    gram = all_sum(gram, (("col", n_col), ("row", n_row)))
    inverse = inverse_factor(gram / F32(d))

    def term_of(at):
        cut = lax.dynamic_slice_in_dim(weight, at * 2 * depth, 2 * depth, 1)
        return dot(cut, full, ((0,), (0,)))

    up_hops = ring // 2
    down_hops = ring - 1 - up_hops
    order = []
    for step in range(up_hops):
        order.append(up_hops - step)
        if step < down_hops:
            order.append(step - down_hops)
    order.append(0)
    terms = {}
    early = None
    for at in order:
        term = term_of((group + at + ring) % ring)
        near = rows_of(term, side * depth, depth)
        away = rows_of(term, (1 - side) * depth, depth)
        if at == up_hops and at:
            early = lax.ppermute(away[half:].astype(BF16), "row", ring_of(n_row))
            got = lax.ppermute(away[:half].astype(BF16), "row", pair_of(n_row))
            near = jnp.concatenate([near[:half] + got.astype(F32), near[half:]], 0)
        else:
            if at == up_hops - 1 and early is not None:
                away = jnp.concatenate([away[:half], away[half:] + early.astype(F32)], 0)
            near = near + lax.ppermute(away.astype(BF16), "row", pair_of(n_row)).astype(F32)
        terms[at] = near

    def travel(hops, sign, pairs):
        moving = None
        for step in range(hops):
            own = terms[sign * (hops - step)]
            if moving is not None:
                own = own + moving.astype(F32)
            moving = lax.ppermute(own.astype(BF16), "row", pairs)
        return moving

    up = travel(up_hops, 1, ring_of(n_row))
    down = travel(down_hops, -1, down_ring)
    factor = terms[0]
    for moved in (up, down):
        if moved is not None:
            factor = factor + moved.astype(F32)

    left_basis = dot(sketch, inverse, ((1,), (1,)), HIGH).astype(BF16)
    right = dot(factor, inverse, ((1,), (1,)), HIGH)
    return left_basis, (right * F32(d ** (-0.5))).astype(BF16)


def solution(mesh):
    n_row, n_col = mesh.shape["row"], mesh.shape["col"]

    def run(weight, basis_prev):
        def body(w, b):
            return per_device(n_row, n_col, weight.shape[0], w, b)

        return jax.shard_map(
            body,
            mesh=mesh,
            in_specs=(P("row", "col"), P(("col", "row"), None)),
            out_specs=(P(("row", "col"), None), P(("col", "row"), None)),
            check_vma=False,
        )(weight, basis_prev)

    return run
```

```python
import functools

import jax
import jax.numpy as jnp
from jax import lax
from jax.experimental import pallas as pl
from jax.experimental.pallas import tpu as pltpu
from jax.sharding import PartitionSpec as P

F32 = jnp.float32
BF16 = jnp.bfloat16
HIGH = lax.Precision.HIGHEST


def dot(a, b, dims, precision=None):
    return lax.dot_general(a, b, ((dims[0], dims[1]), ((), ())), precision=precision,
                           preferred_element_type=F32)


def pair_of(n):
    return [(i, i ^ 1) for i in range(n)]


def ring_of(n):
    return [(i, (i + 2) % n) for i in range(n)]


def rows_of(x, start, count):
    return lax.dynamic_slice_in_dim(x, start, count, 0)


def other_of(index, bit):
    return index + bit - 2 * bit * ((index // bit) % 2)


def gram_sum_kernel(n_row, n_col, gram_ref, out_ref, land_ref, send_sem, recv_sem):
    me, col = lax.axis_index("row"), lax.axis_index("col")
    bits = [1 << i for i in reversed(range(n_col.bit_length() - 1))]
    mesh_id = pl.DeviceIdType.MESH

    barrier = pltpu.get_barrier_semaphore()
    for d in range(1, n_row):
        pl.semaphore_signal(barrier, inc=1, device_id={"row": (me + d) % n_row}, device_id_type=mesh_id)
    for bit in bits:
        pl.semaphore_signal(barrier, inc=1, device_id={"col": other_of(col, bit)}, device_id_type=mesh_id)
    pl.semaphore_wait(barrier, n_row - 1 + len(bits))

    sent = []

    def send(source, target, sem, device):
        copy = pltpu.make_async_remote_copy(
            src_ref=source, dst_ref=target, send_sem=send_sem.at[sem], recv_sem=recv_sem.at[sem],
            device_id=device, device_id_type=mesh_id)
        copy.start()
        sent.append(copy)
        return copy

    first = []
    for d in range(1, n_row):
        peer = (me + d) % n_row
        first.append(send(gram_ref.at[peer], land_ref.at[d - 1], d - 1, {"row": peer}))
    total = gram_ref[me]
    for d in range(1, n_row):
        first[d - 1].wait_recv()
        total = total + land_ref[d - 1]
    out_ref[col, me] = total
    second = []
    for d in range(1, n_row):
        peer = (me + d) % n_row
        second.append(send(out_ref.at[col, me], out_ref.at[col, me], n_row - 2 + d, {"row": peer}))
    for copy in second:
        copy.wait_recv()
    held = [col]
    sem = 2 * (n_row - 1)
    for bit in bits:
        third = []
        for share in held:
            third.append(send(out_ref.at[share], out_ref.at[share], sem, {"col": other_of(col, bit)}))
            sem += 1
        for copy in third:
            copy.wait_recv()
        held = held + [other_of(share, bit) for share in held]
    for copy in sent:
        copy.wait_send()


def gram_sum(share, n_row, n_col):
    rows, n = share.shape
    m = rows // n_row
    count = 2 * (n_row - 1) + n_col - 1
    whole = pl.pallas_call(
        functools.partial(gram_sum_kernel, n_row, n_col),
        out_shape=jax.ShapeDtypeStruct((n_col, n_row, m, n), F32),
        in_specs=[pl.BlockSpec(memory_space=pltpu.VMEM)],
        out_specs=pl.BlockSpec(memory_space=pltpu.VMEM),
        scratch_shapes=[
            pltpu.VMEM((n_row - 1, m, n), F32),
            pltpu.SemaphoreType.DMA((count,)),
            pltpu.SemaphoreType.DMA((count,)),
        ],
        cost_estimate=pl.CostEstimate(flops=20_000_000_000, bytes_accessed=8 * n * n, transcendentals=0),
        compiler_params=pltpu.CompilerParams(
            collective_id=0, has_side_effects=True, vmem_limit_bytes=24 * 2**20),
    )(share.reshape(n_row, m, n))
    return whole.reshape(n, n)


def inverse_kernel(gram_ref, out_ref, work_ref, aug_ref):
    n, b, w = gram_ref.shape[0], 128, 4
    work_ref[...] = gram_ref[...]
    aug_ref[...] = (
        lax.broadcasted_iota(jnp.int32, (n, n), 0) == lax.broadcasted_iota(jnp.int32, (n, n), 1)
    ).astype(F32)
    lane = lax.broadcasted_iota(jnp.int32, (8, b), 1)
    sub = lax.broadcasted_iota(jnp.int32, (8, b), 0)

    def block(i, carry):
        at = pl.ds(pl.multiple_of(i * b, b), b)
        x = [work_ref[pl.ds(pl.multiple_of(i * b + 8 * g, 8), 8), at] for g in range(b // 8)]
        for base in range(0, b, w):
            first = base // 8
            groups = range(first, b // 8)
            wide = {
                (j, g): jnp.broadcast_to(x[g][:, j:j + 1], (8, b))
                for j in range(base, base + w) for g in groups
            }
            for k in range(base, base + w):
                s = k % 8
                over = 1.0 / wide[k, first][s:s + 1]
                row = jnp.where(lane[:1] == k, 1.0, x[first][s:s + 1]) * over
                heads = {j: wide[j, first][s:s + 1] * over for j in range(k + 1, base + w)}
                for g in groups:
                    c = wide[k, g]
                    gone = lane == k
                    if g == first:
                        c = jnp.where(sub > s, c, 0.0)
                        gone = gone & (sub > s)
                    x[g] = jnp.where(gone, 0.0, x[g]) - c * row
                    for j, head in heads.items():
                        wide[j, g] = wide[j, g] - c * head
        rows = []
        for g in range(b // 8):
            here = lane == sub + 8 * g
            pivot = jnp.sum(jnp.where(here, x[g], 0.0), axis=1, keepdims=True)
            unit = jnp.where(lane < sub + 8 * g, x[g], jnp.where(here, 1.0, 0.0))
            rows.append(unit / jnp.sqrt(pivot))
        inv = jnp.concatenate(rows, 0)
        head = dot(inv, work_ref[at, :], ((1,), (0,)), HIGH)
        tail = dot(inv, aug_ref[at, :], ((1,), (0,)), HIGH)
        out_ref[at, :] = tail
        work_ref[...] -= dot(head, head, ((0,), (0,)), HIGH)
        aug_ref[...] -= dot(head, tail, ((0,), (0,)), HIGH)
        return carry

    lax.fori_loop(0, n // b, block, 0)


def inverse_factor(gram):
    n = gram.shape[0]
    return pl.pallas_call(
        inverse_kernel,
        out_shape=jax.ShapeDtypeStruct((n, n), F32),
        in_specs=[pl.BlockSpec(memory_space=pltpu.VMEM)],
        out_specs=pl.BlockSpec(memory_space=pltpu.VMEM),
        scratch_shapes=[pltpu.VMEM((n, n), F32), pltpu.VMEM((n, n), F32)],
        cost_estimate=pl.CostEstimate(flops=20_000_000_000, bytes_accessed=8 * n * n, transcendentals=0),
        compiler_params=pltpu.CompilerParams(vmem_limit_bytes=24 * 2**20),
    )(gram)


def per_device(n_row, n_col, d, weight, basis_prev):
    depth, rank = basis_prev.shape
    me = lax.axis_index("row")
    group, side = me // 2, me % 2
    ring = n_row // 2
    down_ring = [(j, i) for i, j in ring_of(n_row)]

    held = basis_prev
    partial = other = None
    half = depth // 2
    for step in range(ring):
        if step and step + 1 == ring:
            first = lax.ppermute(held[:half], "row", pair_of(n_row))
            second = lax.ppermute(other[half:], "row", ring_of(n_row))
            other = jnp.concatenate([first, second], 0)
        else:
            other = lax.ppermute(held, "row", pair_of(n_row))
        later = lax.ppermute(held, "row", ring_of(n_row)) if step + 1 < ring else None
        owner = (group - step + ring) % ring
        if step + 1 < ring:
            both = jnp.concatenate(
                [jnp.where(side == 0, held, other), jnp.where(side == 0, other, held)], 0)
            cut = lax.dynamic_slice_in_dim(weight, owner * 2 * depth, 2 * depth, 1)
            term = dot(cut, both, ((1,), (0,)))
            partial = term if partial is None else partial + term
        else:
            cut = lax.dynamic_slice_in_dim(weight, (owner * 2 + side) * depth, depth, 1)
            partial = partial + dot(cut, held, ((1,), (0,)))
            partial, other = lax.optimization_barrier((partial, other))
            cut = lax.dynamic_slice_in_dim(weight, (owner * 2 + 1 - side) * depth, depth, 1)
            partial = partial + dot(cut, other, ((1,), (0,)))
        held = later

    rows = weight.shape[0] // n_col
    col = lax.axis_index("col")
    cgroup, cside = col // 2, col % 2
    cring = n_col // 2
    parts = partial.reshape(cring, 2, rows, rank)
    away = lax.dynamic_index_in_dim(parts, 1 - cside, 1, keepdims=False)
    near = lax.dynamic_index_in_dim(parts, cside, 1, keepdims=False)
    near = near + lax.ppermute(away, "col", pair_of(n_col))
    sketch = None
    for step in range(cring):
        at = (cgroup - 1 - step + 2 * cring) % cring
        own = lax.dynamic_index_in_dim(near, at, 0, keepdims=False)
        sketch = own if sketch is None else own + sketch.astype(F32)
        if step + 1 < cring:
            sketch = lax.ppermute(sketch.astype(BF16), "col", ring_of(n_col))

    full = jnp.zeros((cring, 2, rows, rank), BF16)
    held = sketch.astype(BF16)
    for step in range(cring):
        other = lax.ppermute(held, "col", pair_of(n_col))
        later = lax.ppermute(held, "col", ring_of(n_col)) if step + 1 < cring else None
        two = jnp.stack([jnp.where(cside == 0, held, other), jnp.where(cside == 0, other, held)])
        full = lax.dynamic_update_slice(full, two[None], ((cgroup - step + cring) % cring, 0, 0, 0))
        held = later
    full = full.reshape(n_col * rows, rank)

    up_hops = ring // 2
    down_hops = ring - 1 - up_hops
    order = []
    for step in range(up_hops):
        order.append(up_hops - step)
        if step < down_hops:
            order.append(step - down_hops)
    order.append(0)
    share = rank // n_col
    gram = dot(lax.dynamic_slice_in_dim(full, col * share, share, 1), full, ((0,), (0,)))
    gram = gram_sum(gram, n_row, n_col)
    full, gram = lax.optimization_barrier((full, gram))
    terms = {}

    def add_term(at, full, early):
        cut = lax.dynamic_slice_in_dim(weight, (group + at + ring) % ring * 2 * depth, 2 * depth, 1)
        term = dot(cut, full, ((0,), (0,)))
        near = rows_of(term, side * depth, depth)
        away = rows_of(term, (1 - side) * depth, depth)
        if at == up_hops and at:
            early = lax.ppermute(away[half:].astype(BF16), "row", ring_of(n_row))
            got = lax.ppermute(away[:half].astype(BF16), "row", pair_of(n_row))
            near = jnp.concatenate([near[:half] + got.astype(F32), near[half:]], 0)
        else:
            if at == up_hops - 1 and early is not None:
                away = jnp.concatenate([away[:half], away[half:] + early.astype(F32)], 0)
            near = near + lax.ppermute(away.astype(BF16), "row", pair_of(n_row)).astype(F32)
        terms[at] = near
        return early

    def hop(own, moving, pairs):
        if moving is not None:
            own = own + moving.astype(F32)
        return lax.ppermute(own.astype(BF16), "row", pairs)

    early = None
    for at in order[:-1]:
        early = add_term(at, full, early)
    up = down = None
    for step in range(down_hops):
        own = terms[step - down_hops]
        if step == 0:
            own, gram = lax.optimization_barrier((own, gram))
        down = hop(own, down, down_ring)
    inverse = inverse_factor(gram / F32(d))
    for step in range(up_hops):
        own = terms[up_hops - step]
        if step + 1 == up_hops:
            own, inverse = lax.optimization_barrier((own, inverse))
        up = hop(own, up, ring_of(n_row))
    add_term(0, full, early)
    factor = terms[0]
    for moved in (up, down):
        if moved is not None:
            factor = factor + moved.astype(F32)

    left_basis = dot(sketch, inverse, ((1,), (1,)), HIGH).astype(BF16)
    right = dot(factor, inverse, ((1,), (1,)), HIGH)
    return left_basis, (right * F32(d ** (-0.5))).astype(BF16)


def solution(mesh):
    n_row, n_col = mesh.shape["row"], mesh.shape["col"]

    def run(weight, basis_prev):
        def body(w, b):
            return per_device(n_row, n_col, weight.shape[0], w, b)

        return jax.shard_map(
            body,
            mesh=mesh,
            in_specs=(P("row", "col"), P(("col", "row"), None)),
            out_specs=(P(("row", "col"), None), P(("col", "row"), None)),
            check_vma=False,
        )(weight, basis_prev)

    return run
```
